32 devices in a mesh: groups: 2 (over y), row: 4 (over z), col: 4 (over x, core).
Axes of the slice: x: 2, y: 2, z: 4, core: 2. Of those that a mesh axis runs over, the one named last changes fastest.
Arguments:
- hidden: bfloat16 [2048, 8192], P(('groups', 'row'), 'col'), parts along dimension 0, may hold values from -6 to 6
- w_gate_z: bfloat16 [8192, 16384], P('col', 'row'), may hold values from -0.0625 to 0.0625
- w_input_x: bfloat16 [8192, 16384], P('col', 'row'), may hold values from -0.0625 to 0.0625
- w_input_bc: bfloat16 [8192, 4096], P('col', 'row'), may hold values from -0.0625 to 0.0625
- w_input_dt: bfloat16 [8192, 256], P('col', 'row'), may hold values from -0.0625 to 0.0625
- conv_kernel_x: bfloat16 [4, 16384], P(None, 'row'), may hold values from -3 to 3
- conv_kernel_bc: bfloat16 [4, 4096], P(None, 'row'), may hold values from -3 to 3
- conv_state_x: bfloat16 [6, 16384], P('groups', 'row'), parts along dimension 0, may hold values from -6 to 6
- conv_state_bc: bfloat16 [6, 4096], P('groups', 'row'), parts along dimension 0, may hold values from -6 to 6
- dt_bias: float32 [256], P('row'), may hold values from -5 to -3
- a_log: float32 [256], P('row'), may hold values from -3 to 1.1
- d_skip: float32 [256], P('row'), may hold values from 0.5 to 1.5
- norm_gain: float32 [16384], P('row'), may hold values from 0.1 to 1.9
- ssm_state: float32 [512, 64, 256], P(('groups', 'row')), parts along dimension 0, may hold values from -6 to 6
- w_output: bfloat16 [16384, 8192], P('row', 'col'), may hold values from -0.046875 to 0.046875
Outputs:
- mixed: bfloat16 [2048, 8192], P(('groups', 'row'), 'col'), parts along dimension 0
The draws below stay inside these ranges and needn't reach their ends.
There are 2 independent parts, one for each index of `groups`. The reference program is written for one: setup_inputs(seed, part) draws one part's arguments, and reference() takes and returns one part's arrays. A program takes and returns all parts, laid end to end along the dimension named above; an argument that names none is the same for every part. Nothing has to cross between parts.
All inputs are finite; a program needn't handle non-finite values.
Results may differ from the reference program's by a relative error of at most 0.02.
Values may be sent and summed in bfloat16 or wider, within the bound.
A program may use at most 256 MiB of HBM per device.

```python
import jax
import jax.numpy as jnp
from jax import lax

D = 8192
H = 256
P_SIZE = 64
NS = 256
G = 8
KW = 4
L = 1024
DI = 16384
DCOL = 2048
CR = 4096


def block_scale(key, extent, pieces, low, largest):
    gain = 1.0
    for dim, shards_of in pieces:
        draws = jax.random.uniform(jax.random.fold_in(jax.random.fold_in(key, 6), dim), (shards_of,), jnp.float32, low / len(pieces), largest / len(pieces))
        gain = gain * jnp.repeat(jnp.exp(draws), extent[dim] // shards_of).reshape((-1,) + (1,) * (len(extent) - 1 - dim))
    return gain


def noise(rng, shape, spread, bound, split=(), held_as=jnp.bfloat16):
    entries = spread * jax.random.normal(rng, shape, jnp.float32)
    if split:
        entries = entries * block_scale(rng, shape, split, -0.22, 0.18)
    return jnp.clip(entries, -bound, bound).astype(held_as)


def setup_inputs(seed: int = 0, part: int = 0) -> dict:
    splits = jax.random.split(jax.random.key(seed), 16)
    own_keys = jax.random.split(jax.random.fold_in(splits[15], part), 16)
    hidden = noise(own_keys[0], (L, D), 1.0, 6.0, ((0, 4), (1, 4)))
    w_gate_z = noise(splits[1], (D, DI), D ** -0.5, 0.0625, ((0, 4), (1, 4)))
    w_input_x = noise(splits[2], (D, DI), D ** -0.5, 0.0625, ((0, 4), (1, 4)))
    w_input_bc = noise(splits[3], (D, 2 * G * NS), D ** -0.5, 0.0625, ((0, 4), (1, 4)))
    w_input_dt = noise(splits[4], (D, H), D ** -0.5, 0.0625, ((0, 4), (1, 4)))
    conv_kernel_x = noise(splits[5], (KW, DI), 0.5, 3.0, ((1, 4),))
    conv_kernel_bc = noise(splits[6], (KW, 2 * G * NS), 0.5, 3.0, ((1, 4),))
    conv_state_x = noise(own_keys[7], (KW - 1, DI), 1.0, 6.0, ((1, 4),))
    conv_state_bc = noise(own_keys[8], (KW - 1, 2 * G * NS), 1.0, 6.0, ((1, 4),))
    dt_bias = jnp.clip(-5.0 + 2.0 * jax.random.uniform(splits[9], (H,), jnp.float32) ** block_scale(splits[9], (H,), ((0, 4),), -0.2, 0.2), -5.0, -3.0)
    a_log = jnp.clip(-3.0 + 4.1 * jax.random.uniform(splits[10], (H,), jnp.float32) ** block_scale(splits[10], (H,), ((0, 4),), -0.2, 0.2), -3.0, 1.1)
    d_skip = jnp.clip(0.5 + 1.0 * jax.random.uniform(splits[11], (H,), jnp.float32) ** block_scale(splits[11], (H,), ((0, 4),), -0.2, 0.2), 0.5, 1.5)
    norm_gain = jnp.clip(1.0 + 0.18 * jax.random.normal(splits[12], (DI,), jnp.float32), 0.1, 1.9)
    ssm_state = noise(own_keys[13], (H, P_SIZE, NS), 1.0, 6.0, ((0, 4),), jnp.float32)
    w_output = noise(splits[14], (DI, D), DI ** -0.5, 0.046875, ((0, 4), (1, 4)))
    return {"hidden": hidden, "w_gate_z": w_gate_z, "w_input_x": w_input_x, "w_input_bc": w_input_bc, "w_input_dt": w_input_dt, "conv_kernel_x": conv_kernel_x, "conv_kernel_bc": conv_kernel_bc, "conv_state_x": conv_state_x, "conv_state_bc": conv_state_bc, "dt_bias": dt_bias, "a_log": a_log, "d_skip": d_skip, "norm_gain": norm_gain, "ssm_state": ssm_state, "w_output": w_output}


def convolve_silu(previous, current, kernel):
    stacked = jnp.concatenate([previous, current], axis=0).astype(jnp.float32)
    length = current.shape[0]
    accum = jnp.zeros(current.shape, jnp.float32)
    for offset in range(kernel.shape[0]):
        accum = accum + kernel[offset].astype(jnp.float32)[None, :] * stacked[offset:offset + length]
    return jax.nn.silu(accum).astype(jnp.bfloat16)

def reference(hidden, w_gate_z, w_input_x, w_input_bc, w_input_dt, conv_kernel_x, conv_kernel_bc, conv_state_x, conv_state_bc, dt_bias, a_log, d_skip, norm_gain, ssm_state, w_output):
    weights = jnp.concatenate([w_gate_z, w_input_x, w_input_bc, w_input_dt], axis=1)
    summed = jnp.zeros((L, weights.shape[1]), jnp.float32)
    for block_idx in range(D // DCOL):
        partial_sum = jnp.dot(hidden[:, block_idx * DCOL:(block_idx + 1) * DCOL], weights[block_idx * DCOL:(block_idx + 1) * DCOL], preferred_element_type=jnp.float32)
        rounded = lax.optimization_barrier(partial_sum.astype(jnp.bfloat16))
        summed = summed + rounded.astype(jnp.float32)
    bc_width = 2 * G * NS
    gate_z = summed[:, :DI].astype(jnp.bfloat16)
    input_x = summed[:, DI:2 * DI].astype(jnp.bfloat16)
    input_bc = summed[:, 2 * DI:2 * DI + bc_width].astype(jnp.bfloat16)
    dt_raw = summed[:, 2 * DI + bc_width:]
    conv_x = convolve_silu(conv_state_x, input_x, conv_kernel_x)
    conv_bc = convolve_silu(conv_state_bc, input_bc, conv_kernel_bc)
    steps_dt = jax.nn.softplus(dt_raw + dt_bias[None, :])
    log_decay = steps_dt * (-jnp.exp(a_log))[None, :]
    per_group = H // G
    b_groups = conv_bc[:, :G * NS].astype(jnp.float32).reshape(L, G, NS)
    c_groups = conv_bc[:, G * NS:].astype(jnp.float32).reshape(L, G, NS)
    b_heads = jnp.repeat(b_groups, per_group, axis=1)
    c_heads = jnp.repeat(c_groups, per_group, axis=1)
    x_heads = conv_x.astype(jnp.float32).reshape(L, H, P_SIZE)

    def advance(state, inputs):
        x_tok, b_tok, c_tok, dt_tok, log_tok = inputs
        state = jnp.exp(log_tok)[:, None, None] * state + (dt_tok[:, None] * x_tok)[:, :, None] * b_tok[:, None, :]
        output = jnp.einsum('hpn,hn->hp', state, c_tok, precision=lax.Precision.HIGHEST)
        return (state, output)
    outputs = lax.scan(advance, ssm_state.astype(jnp.float32), (x_heads, b_heads, c_heads, steps_dt, log_decay))[1]
    y_heads = outputs + d_skip[None, :, None] * x_heads
    gated = y_heads.reshape(L, DI) * jax.nn.silu(gate_z.astype(jnp.float32))
    grouped = gated.reshape(L, G, DI // G)
    mean_sq = lax.optimization_barrier(jnp.mean(grouped * grouped, axis=2, keepdims=True))
    normed = (grouped * lax.rsqrt(mean_sq + 1e-05)).reshape(L, DI)
    y_normed = (normed * norm_gain[None, :]).astype(jnp.bfloat16)
    result = jnp.zeros((L, D), jnp.float32)
    for block_idx in range(DI // CR):
        partial_sum = jnp.dot(y_normed[:, block_idx * CR:(block_idx + 1) * CR], w_output[block_idx * CR:(block_idx + 1) * CR], preferred_element_type=jnp.float32)
        rounded = lax.optimization_barrier(partial_sum.astype(jnp.bfloat16))
        result = result + rounded.astype(jnp.float32)
    return result.astype(jnp.bfloat16)
```

```python
import jax
import jax.numpy as jnp
from jax import lax
from jax.experimental import pallas as pl
from jax.experimental.pallas import tpu as pltpu
from jax.sharding import PartitionSpec as P

highest = lax.Precision.HIGHEST


def from_behind(value, axis, steps):
    count = lax.axis_size(axis)
    first, last = (max(0, -steps), min(count, count - steps))
    return lax.ppermute(value, axis, [(source, source + steps) for source in range(first, last)])


def entering(value, axis, combine, identity):
    count, mine = (lax.axis_size(axis), lax.axis_index(axis))
    everything = jax.tree.map(
        lambda part, kind: lax.all_gather(part.astype(kind), axis),
        value,
        (jnp.bfloat16, jnp.bfloat16),
    )
    start = jax.tree.map(
        lambda part, zero: jnp.broadcast_to(jnp.asarray(zero, part.dtype), part.shape),
        value,
        identity,
    )

    def turn(k, before):
        reached = k < mine
        new = combine(
            before, jax.tree.map(lambda part, own: part[k].astype(own.dtype), everything, value)
        )
        return jax.tree.map(lambda a, b: jnp.where(reached, a, b), new, before)

    return lax.fori_loop(0, count, turn, start)


def swapped(value, axis, bit):
    mask = 2**bit
    pairs = [(source, source ^ mask) for source in range(lax.axis_size(axis))]
    return lax.ppermute(value, axis, pairs)


def convolve_silu(previous, current, kernel):
    stacked = jnp.concatenate([previous, current], axis=0).astype(jnp.float32)
    length = current.shape[0]
    accum = jnp.zeros(current.shape, jnp.float32)
    for offset in range(kernel.shape[0]):
        accum = (
            accum + kernel[offset].astype(jnp.float32)[None, :] * stacked[offset : offset + length]
        )
    return jax.nn.silu(accum).astype(jnp.bfloat16)


def block_parts(x_block, b_block, c_block, dt_block, log_block):
    length = x_block.shape[0]
    cumulative = jnp.cumsum(log_block, axis=0)
    scores = jnp.einsum("tjn,sjn->jts", c_block, b_block, precision=highest)
    spans = cumulative.T[:, :, None] - cumulative.T[:, None, :]
    causal = (jnp.arange(length)[:, None] >= jnp.arange(length)[None, :])[None, :, :]
    decay_mask = jnp.where(causal, jnp.exp(jnp.where(causal, spans, 0.0)), 0.0)
    mixing = scores * decay_mask * dt_block.T[:, None, :]
    intra = jnp.einsum("jts,sjp->tjp", mixing, x_block, precision=highest)
    tail_weight = jnp.exp(cumulative[-1][None, :] - cumulative) * dt_block
    local_state = jnp.einsum("sj,sjp,sjn->jpn", tail_weight, x_block, b_block, precision=highest)
    return (intra, cumulative, local_state)


def local_scan(x_heads, b_heads, c_heads, steps_dt, log_decay):
    length, heads_here, head_size = x_heads.shape
    state_size = b_heads.shape[2]
    block_len = min(length, 256)
    blocks = length // block_len

    def to_blocks(array):
        return array.reshape((blocks, block_len) + array.shape[1:])

    def advance(carry_state, inputs):
        x_block, b_block, c_block, dt_block, log_block = inputs
        intra, cumulative, local_state = block_parts(x_block, b_block, c_block, dt_block, log_block)
        carried = jnp.exp(cumulative)[:, :, None] * jnp.einsum(
            "tjn,jpn->tjp", c_block, carry_state, precision=highest
        )
        new_state = jnp.exp(cumulative[-1])[:, None, None] * carry_state + local_state
        return (new_state, intra + carried)

    initial = jnp.zeros((heads_here, head_size, state_size), jnp.float32)
    final_state, outputs = lax.scan(
        advance,
        initial,
        (
            to_blocks(x_heads),
            to_blocks(b_heads),
            to_blocks(c_heads),
            to_blocks(steps_dt),
            to_blocks(log_decay),
        ),
    )
    return (outputs.reshape(length, heads_here, head_size), final_state)


def chain_combine(earlier, later_part):
    return (earlier[0] * later_part[0], later_part[0][:, None, None] * earlier[1] + later_part[1])


def general(
    hidden,
    w_gate_z,
    w_input_x,
    w_input_bc,
    w_input_dt,
    conv_kernel_x,
    conv_kernel_bc,
    conv_state_x,
    conv_state_bc,
    dt_bias,
    a_log,
    d_skip,
    norm_gain,
    ssm_state,
    w_output,
):
    channels = w_gate_z.shape[1]
    bc_local = w_input_bc.shape[1]
    heads_local = w_input_dt.shape[1]
    head_size = ssm_state.shape[1]
    state_size = ssm_state.shape[2]
    kernel_len = conv_kernel_x.shape[0]
    weights = jnp.concatenate([w_gate_z, w_input_x, w_input_bc, w_input_dt], axis=1)
    partial_proj = jnp.dot(
        lax.all_gather(hidden, "row", axis=0, tiled=True),
        weights,
        preferred_element_type=jnp.float32,
    )
    summed = lax.psum_scatter(
        partial_proj.astype(jnp.bfloat16), "col", scatter_dimension=0, tiled=True
    ).astype(jnp.float32)
    gate_z = summed[:, :channels].astype(jnp.bfloat16)
    input_x = summed[:, channels : 2 * channels].astype(jnp.bfloat16)
    input_bc = summed[:, 2 * channels : 2 * channels + bc_local].astype(jnp.bfloat16)
    dt_raw = summed[:, 2 * channels + bc_local :]
    tail_rows = jnp.concatenate(
        [input_x[-(kernel_len - 1) :], input_bc[-(kernel_len - 1) :]], axis=1
    )
    arrived = from_behind(tail_rows, "col", 1)
    first_col = lax.axis_index("col") == 0
    prev_x = jnp.where(first_col, conv_state_x, arrived[:, :channels])
    prev_bc = jnp.where(first_col, conv_state_bc, arrived[:, channels:])
    conv_x = convolve_silu(prev_x, input_x, conv_kernel_x)
    conv_bc = convolve_silu(prev_bc, input_bc, conv_kernel_bc)
    tokens_here = conv_x.shape[0]
    gathered_bc = lax.all_gather(conv_bc, "row", axis=1, tiled=True)
    bc_total = gathered_bc.shape[1]
    group_count = bc_total // (2 * state_size)
    heads_total = heads_local * lax.axis_size("row")
    per_group = heads_total // group_count
    head_ids = lax.axis_index("row") * heads_local + jnp.arange(heads_local, dtype=jnp.int32)
    group_ids = head_ids // per_group
    onehot = group_ids[:, None] == jnp.arange(group_count, dtype=jnp.int32)[None, :]
    b_groups = gathered_bc[:, : bc_total // 2].reshape(tokens_here, group_count, state_size)
    c_groups = gathered_bc[:, bc_total // 2 :].reshape(tokens_here, group_count, state_size)
    b_heads = jnp.einsum(
        "tgn,jg->tjn", b_groups, onehot.astype(jnp.bfloat16), preferred_element_type=jnp.float32
    )
    c_heads = jnp.einsum(
        "tgn,jg->tjn", c_groups, onehot.astype(jnp.bfloat16), preferred_element_type=jnp.float32
    )
    steps_dt = jax.nn.softplus(dt_raw + dt_bias[None, :])
    log_decay = steps_dt * (-jnp.exp(a_log))[None, :]
    x_heads = conv_x.astype(jnp.float32).reshape(tokens_here, heads_local, head_size)
    local_out, local_state = local_scan(x_heads, b_heads, c_heads, steps_dt, log_decay)
    cumulative = jnp.cumsum(log_decay, axis=0)
    decay_total = jnp.exp(cumulative[-1])
    prefix_decay, prefix_state = entering(
        (decay_total, local_state),
        "col",
        chain_combine,
        (jnp.ones_like(decay_total), jnp.zeros_like(local_state)),
    )
    incoming = prefix_state + prefix_decay[:, None, None] * ssm_state
    carried = jnp.exp(cumulative)[:, :, None] * jnp.einsum(
        "tjn,jpn->tjp", c_heads, incoming, precision=highest
    )
    y_heads = local_out + carried + d_skip[None, :, None] * x_heads
    gated = y_heads * jax.nn.silu(gate_z.astype(jnp.float32)).reshape(
        tokens_here, heads_local, head_size
    )
    head_squares = jnp.sum(gated * gated, axis=2)
    if per_group <= heads_local:
        group_sums = jnp.sum(
            head_squares.reshape(tokens_here, heads_local // per_group, per_group), axis=2
        )
        head_mean = jnp.repeat(group_sums, per_group, axis=1) / (per_group * head_size)
    else:
        partial_squares = jnp.sum(head_squares, axis=1, keepdims=True)
        for bit_number in range((per_group // heads_local).bit_length() - 1):
            partial_squares = partial_squares + swapped(partial_squares, "row", bit_number)
        head_mean = jnp.broadcast_to(partial_squares, (tokens_here, heads_local)) / (
            per_group * head_size
        )
    normed = gated * lax.rsqrt(head_mean + 1e-05)[:, :, None]
    y_normed = (normed.reshape(tokens_here, channels) * norm_gain[None, :]).astype(jnp.bfloat16)
    all_tokens = lax.all_gather(y_normed, "col", axis=0, tiled=True)
    return lax.psum_scatter(
        jnp.dot(all_tokens, w_output, preferred_element_type=jnp.float32).astype(jnp.bfloat16),
        "row",
        scatter_dimension=0,
        tiled=True,
    )


def scan_kernel(x_ref, b_ref, c_ref, dt_ref, cum_ref, dt_t_ref, cum_t_ref, skip_ref, first_ref, y_ref, state):
    heads = dt_ref.shape[1]
    size = x_ref.shape[1] // heads
    length = x_ref.shape[0]

    @pl.when(pl.program_id(0) == 0)
    def _():
        state[...] = first_ref[...]

    b = b_ref[...]
    c = c_ref[...]
    contract_last = (((1,), (1,)), ((), ()))
    scores = lax.dot_general(c, b, contract_last, preferred_element_type=jnp.float32)
    rows = lax.broadcasted_iota(jnp.int32, (length, length), 0)
    cols = lax.broadcasted_iota(jnp.int32, (length, length), 1)
    causal = rows >= cols
    scores = jnp.where(causal, scores, 0.0)
    carried = lax.dot_general(
        c, state[...].astype(jnp.bfloat16), contract_last, preferred_element_type=jnp.float32
    )
    outs = []
    weighted = []
    for h in range(heads):
        at = slice(h * size, (h + 1) * size)
        x = x_ref[:, at]
        xf = x.astype(jnp.float32)
        cum = cum_ref[:, h : h + 1]
        cum_t = cum_t_ref[h : h + 1, :]
        last = cum_t[:, length - 1 : length]
        mixing = scores * jnp.exp(jnp.minimum(cum - cum_t, 0.0)) * dt_t_ref[h : h + 1, :]
        intra = jnp.dot(mixing.astype(jnp.bfloat16), x, preferred_element_type=jnp.float32)
        outs.append(
            intra + jnp.exp(cum) * carried[:, at] + skip_ref[h : h + 1, 0:1] * xf
        )
        weighted.append((xf * (jnp.exp(last - cum) * dt_ref[:, h : h + 1])).astype(jnp.bfloat16))
    for h in range(0, heads, 2):
        y_ref[:, h * size : (h + 2) * size] = jnp.concatenate(outs[h : h + 2], axis=1)
    added = lax.dot_general(
        jnp.concatenate(weighted, axis=1),
        b,
        (((0,), (0,)), ((), ())),
        preferred_element_type=jnp.float32,
    )
    for h in range(heads):
        at = slice(h * size, (h + 1) * size)
        decay = jnp.exp(cum_t_ref[h : h + 1, length - 1 : length])
        state[at, :] = decay * state[at, :] + added[at, :]


def scan_heads(x, b, c, dt_t, cum_t, skip, first, block):
    tokens, width = x.shape
    heads, n = dt_t.shape[0], b.shape[1]
    by_rows = lambda w: pl.BlockSpec((block, w), lambda i: (i, 0))
    by_cols = pl.BlockSpec((heads, block), lambda i: (0, i))
    return pl.pallas_call(
        scan_kernel,
        grid=(tokens // block,),
        in_specs=[
            by_rows(width),
            by_rows(n),
            by_rows(n),
            by_rows(heads),
            by_rows(heads),
            by_cols,
            by_cols,
            pl.BlockSpec((heads, 128), lambda i: (0, 0)),
            pl.BlockSpec((width, n), lambda i: (0, 0)),
        ],
        out_specs=by_rows(width),
        out_shape=jax.ShapeDtypeStruct((tokens, width), jnp.float32),
        scratch_shapes=[pltpu.VMEM((width, n), jnp.float32)],
        compiler_params=pltpu.CompilerParams(vmem_limit_bytes=40 * 2**20),
        cost_estimate=pl.CostEstimate(
            flops=2 * tokens * (block * width + 2 * width * n),
            bytes_accessed=8 * tokens * width,
            transcendentals=tokens * block * heads,
        ),
    )(x, b, c, dt_t.T, cum_t.T, dt_t, cum_t, jnp.broadcast_to(skip[:, None], (heads, 128)), first)


def scatter_channels(partial, dim):
    mine = lax.axis_index("col")
    core, chip = mine % 2, mine // 2
    step = partial.shape[dim] // 4

    def block(array, k, width):
        return lax.dynamic_slice_in_dim(array, k * width, width, dim)

    give = [block(partial, 2 * k + 1 - core, step) for k in range(2)]
    keep = [block(partial, 2 * k + core, step) for k in range(2)]
    got = swapped(jnp.concatenate(give, axis=dim), "col", 0)
    got = [lax.slice_in_dim(got, k * step, (k + 1) * step, axis=dim) for k in range(2)]
    pair = [a.astype(jnp.float32) + b.astype(jnp.float32) for a, b in zip(keep, got)]
    far = jnp.where(chip == 0, pair[1], pair[0]).astype(jnp.bfloat16)
    near = jnp.where(chip == 0, pair[0], pair[1]).astype(jnp.bfloat16)
    return near.astype(jnp.float32) + swapped(far, "col", 1).astype(jnp.float32)


def by_heads(
    hidden,
    w_gate_z,
    w_input_x,
    w_input_bc,
    w_input_dt,
    conv_kernel_x,
    conv_kernel_bc,
    conv_state_x,
    conv_state_bc,
    dt_bias,
    a_log,
    d_skip,
    norm_gain,
    ssm_state,
    w_output,
):
    row, col = lax.axis_index("row"), lax.axis_index("col")
    cols = lax.axis_size("col")
    rows = lax.axis_size("row")
    channels = w_gate_z.shape[1] // cols
    bc_width = w_input_bc.shape[1] // cols
    heads = w_input_dt.shape[1] // cols
    head_size, state_size = ssm_state.shape[1:]

    def share(array, dim):
        width = array.shape[dim] // cols
        return lax.dynamic_slice_in_dim(array, col * width, width, dim)

    tokens = lax.all_gather(hidden, "row", axis=0, tiled=True)
    length = tokens.shape[0]

    def project(weights):
        return jnp.dot(tokens, weights, preferred_element_type=jnp.float32).astype(jnp.bfloat16)

    part_bc = project(w_input_bc)
    part_dt = lax.dot_general(
        w_input_dt, tokens, (((0,), (1,)), ((), ())), preferred_element_type=jnp.float32
    ).astype(jnp.bfloat16)
    part_x = project(w_input_x)
    part_z = project(w_gate_z)
    input_bc = scatter_channels(part_bc, 1).astype(jnp.bfloat16)
    dt_raw = scatter_channels(part_dt, 0)
    input_x = scatter_channels(part_x, 1).astype(jnp.bfloat16)
    gate_z = scatter_channels(part_z, 1).astype(jnp.bfloat16)

    conv_bc = convolve_silu(share(conv_state_bc, 1), input_bc, share(conv_kernel_bc, 1))
    routes = []
    for r in range(rows):
        for c in range(cols):
            group = (r * cols + c) // 2
            source = group + (c % 2) * (rows * cols // 2)
            routes.append((source, r * cols + c))
    own = lax.ppermute(conv_bc, ("row", "col"), routes)
    other = swapped(own, "col", 0)
    even = col % 2 == 0
    b = jnp.where(even, own, other)
    c = jnp.where(even, other, own)

    block = 256
    steps_dt = jax.nn.softplus(dt_raw + share(dt_bias, 0)[:, None])
    log_decay = steps_dt * (-jnp.exp(share(a_log, 0)))[:, None]
    upper = (jnp.arange(block)[:, None] <= jnp.arange(block)[None, :]).astype(jnp.float32)
    cum = jnp.einsum(
        "hks,st->hkt", log_decay.reshape(heads, length // block, block), upper, precision=highest
    ).reshape(heads, length)
    conv_x = convolve_silu(share(conv_state_x, 1), input_x, share(conv_kernel_x, 1))
    first = share(ssm_state, 0).reshape(heads * head_size, state_size)
    y = scan_heads(conv_x, b, c, steps_dt, cum, share(d_skip, 0), first, block)

    gated = y * jax.nn.silu(gate_z.astype(jnp.float32))
    squares = jnp.sum(gated * gated, axis=1)
    squares = squares + swapped(squares, "col", 0)
    scale = lax.rsqrt(squares / (2 * channels) + 1e-05)
    normed = (gated * scale[:, None] * share(norm_gain, 0)[None, :]).astype(jnp.bfloat16)

    across = swapped(normed, "col", 1)
    beside = swapped(normed, "col", 0)
    corner = swapped(across, "col", 0)

    def rows_of(k):
        return lax.dynamic_slice_in_dim(w_output, k * channels, channels, 0)

    mixed = jnp.zeros((length, w_output.shape[1]), jnp.float32)
    for piece, mask in ((normed, 0), (beside, 1), (across, 2), (corner, 3)):
        mixed = mixed + jnp.dot(piece, rows_of(col ^ mask), preferred_element_type=jnp.float32)
    return lax.psum_scatter(
        mixed.astype(jnp.bfloat16), "row", scatter_dimension=0, tiled=True
    )


def local(*arrays):
    w_gate_z, w_input_bc, w_input_dt, ssm_state = arrays[1], arrays[3], arrays[4], arrays[13]
    rows, cols = lax.axis_size("row"), lax.axis_size("col")
    tokens = arrays[0].shape[0] * rows
    state_size = ssm_state.shape[2]
    groups = w_input_bc.shape[1] * rows // (2 * state_size)
    fits = (
        cols == 4
        and w_input_bc.shape[1] == cols * state_size
        and groups * 2 == rows * cols
        and w_input_dt.shape[1] % (2 * cols) == 0
        and w_gate_z.shape[1] % (cols * 128) == 0
        and tokens % 256 == 0
    )
    return by_heads(*arrays) if fits else general(*arrays)


def solution(mesh):
    return jax.shard_map(
        local,
        mesh=mesh,
        in_specs=(
            P(("groups", "row"), "col"),
            P("col", "row"),
            P("col", "row"),
            P("col", "row"),
            P("col", "row"),
            P(None, "row"),
            P(None, "row"),
            P("groups", "row"),
            P("groups", "row"),
            P("row"),
            P("row"),
            P("row"),
            P("row"),
            P(("groups", "row"), None, None),
            P("row", "col"),
        ),
        out_specs=P(("groups", "row"), "col"),
        check_vma=False,
    )
```

```python
import jax
import jax.numpy as jnp
from jax import lax
from jax.experimental import pallas as pl
from jax.experimental.pallas import tpu as pltpu
from jax.sharding import PartitionSpec as P

highest = lax.Precision.HIGHEST


def from_behind(value, axis, steps):
    count = lax.axis_size(axis)
    first, last = (max(0, -steps), min(count, count - steps))
    return lax.ppermute(value, axis, [(source, source + steps) for source in range(first, last)])


def entering(value, axis, combine, identity):
    count, mine = (lax.axis_size(axis), lax.axis_index(axis))
    everything = jax.tree.map(
        lambda part, kind: lax.all_gather(part.astype(kind), axis),
        value,
        (jnp.bfloat16, jnp.bfloat16),
    )
    start = jax.tree.map(
        lambda part, zero: jnp.broadcast_to(jnp.asarray(zero, part.dtype), part.shape),
        value,
        identity,
    )

    def turn(k, before):
        reached = k < mine
        new = combine(
            before, jax.tree.map(lambda part, own: part[k].astype(own.dtype), everything, value)
        )
        return jax.tree.map(lambda a, b: jnp.where(reached, a, b), new, before)

    return lax.fori_loop(0, count, turn, start)


def swapped(value, axis, bit):
    mask = 2**bit
    pairs = [(source, source ^ mask) for source in range(lax.axis_size(axis))]
    return lax.ppermute(value, axis, pairs)


def convolve_silu(previous, current, kernel):
    stacked = jnp.concatenate([previous, current], axis=0).astype(jnp.float32)
    length = current.shape[0]
    accum = jnp.zeros(current.shape, jnp.float32)
    for offset in range(kernel.shape[0]):
        accum = (
            accum + kernel[offset].astype(jnp.float32)[None, :] * stacked[offset : offset + length]
        )
    return jax.nn.silu(accum).astype(jnp.bfloat16)


def block_parts(x_block, b_block, c_block, dt_block, log_block):
    length = x_block.shape[0]
    cumulative = jnp.cumsum(log_block, axis=0)
    scores = jnp.einsum("tjn,sjn->jts", c_block, b_block, precision=highest)
    spans = cumulative.T[:, :, None] - cumulative.T[:, None, :]
    causal = (jnp.arange(length)[:, None] >= jnp.arange(length)[None, :])[None, :, :]
    decay_mask = jnp.where(causal, jnp.exp(jnp.where(causal, spans, 0.0)), 0.0)
    mixing = scores * decay_mask * dt_block.T[:, None, :]
    intra = jnp.einsum("jts,sjp->tjp", mixing, x_block, precision=highest)
    tail_weight = jnp.exp(cumulative[-1][None, :] - cumulative) * dt_block
    local_state = jnp.einsum("sj,sjp,sjn->jpn", tail_weight, x_block, b_block, precision=highest)
    return (intra, cumulative, local_state)


def local_scan(x_heads, b_heads, c_heads, steps_dt, log_decay):
    length, heads_here, head_size = x_heads.shape
    state_size = b_heads.shape[2]
    block_len = min(length, 256)
    blocks = length // block_len

    def to_blocks(array):
        return array.reshape((blocks, block_len) + array.shape[1:])

    def advance(carry_state, inputs):
        x_block, b_block, c_block, dt_block, log_block = inputs
        intra, cumulative, local_state = block_parts(x_block, b_block, c_block, dt_block, log_block)
        carried = jnp.exp(cumulative)[:, :, None] * jnp.einsum(
            "tjn,jpn->tjp", c_block, carry_state, precision=highest
        )
        new_state = jnp.exp(cumulative[-1])[:, None, None] * carry_state + local_state
        return (new_state, intra + carried)

    initial = jnp.zeros((heads_here, head_size, state_size), jnp.float32)
    final_state, outputs = lax.scan(
        advance,
        initial,
        (
            to_blocks(x_heads),
            to_blocks(b_heads),
            to_blocks(c_heads),
            to_blocks(steps_dt),
            to_blocks(log_decay),
        ),
    )
    return (outputs.reshape(length, heads_here, head_size), final_state)


def chain_combine(earlier, later_part):
    return (earlier[0] * later_part[0], later_part[0][:, None, None] * earlier[1] + later_part[1])


def general(
    hidden,
    w_gate_z,
    w_input_x,
    w_input_bc,
    w_input_dt,
    conv_kernel_x,
    conv_kernel_bc,
    conv_state_x,
    conv_state_bc,
    dt_bias,
    a_log,
    d_skip,
    norm_gain,
    ssm_state,
    w_output,
):
    channels = w_gate_z.shape[1]
    bc_local = w_input_bc.shape[1]
    heads_local = w_input_dt.shape[1]
    head_size = ssm_state.shape[1]
    state_size = ssm_state.shape[2]
    kernel_len = conv_kernel_x.shape[0]
    weights = jnp.concatenate([w_gate_z, w_input_x, w_input_bc, w_input_dt], axis=1)
    partial_proj = jnp.dot(
        lax.all_gather(hidden, "row", axis=0, tiled=True),
        weights,
        preferred_element_type=jnp.float32,
    )
    summed = lax.psum_scatter(
        partial_proj.astype(jnp.bfloat16), "col", scatter_dimension=0, tiled=True
    ).astype(jnp.float32)
    gate_z = summed[:, :channels].astype(jnp.bfloat16)
    input_x = summed[:, channels : 2 * channels].astype(jnp.bfloat16)
    input_bc = summed[:, 2 * channels : 2 * channels + bc_local].astype(jnp.bfloat16)
    dt_raw = summed[:, 2 * channels + bc_local :]
    tail_rows = jnp.concatenate(
        [input_x[-(kernel_len - 1) :], input_bc[-(kernel_len - 1) :]], axis=1
    )
    arrived = from_behind(tail_rows, "col", 1)
    first_col = lax.axis_index("col") == 0
    prev_x = jnp.where(first_col, conv_state_x, arrived[:, :channels])
    prev_bc = jnp.where(first_col, conv_state_bc, arrived[:, channels:])
    conv_x = convolve_silu(prev_x, input_x, conv_kernel_x)
    conv_bc = convolve_silu(prev_bc, input_bc, conv_kernel_bc)
    tokens_here = conv_x.shape[0]
    gathered_bc = lax.all_gather(conv_bc, "row", axis=1, tiled=True)
    bc_total = gathered_bc.shape[1]
    group_count = bc_total // (2 * state_size)
    heads_total = heads_local * lax.axis_size("row")
    per_group = heads_total // group_count
    head_ids = lax.axis_index("row") * heads_local + jnp.arange(heads_local, dtype=jnp.int32)
    group_ids = head_ids // per_group
    onehot = group_ids[:, None] == jnp.arange(group_count, dtype=jnp.int32)[None, :]
    b_groups = gathered_bc[:, : bc_total // 2].reshape(tokens_here, group_count, state_size)
    c_groups = gathered_bc[:, bc_total // 2 :].reshape(tokens_here, group_count, state_size)
    b_heads = jnp.einsum(
        "tgn,jg->tjn", b_groups, onehot.astype(jnp.bfloat16), preferred_element_type=jnp.float32
    )
    c_heads = jnp.einsum(
        "tgn,jg->tjn", c_groups, onehot.astype(jnp.bfloat16), preferred_element_type=jnp.float32
    )
    steps_dt = jax.nn.softplus(dt_raw + dt_bias[None, :])
    log_decay = steps_dt * (-jnp.exp(a_log))[None, :]
    x_heads = conv_x.astype(jnp.float32).reshape(tokens_here, heads_local, head_size)
    local_out, local_state = local_scan(x_heads, b_heads, c_heads, steps_dt, log_decay)
    cumulative = jnp.cumsum(log_decay, axis=0)
    decay_total = jnp.exp(cumulative[-1])
    prefix_decay, prefix_state = entering(
        (decay_total, local_state),
        "col",
        chain_combine,
        (jnp.ones_like(decay_total), jnp.zeros_like(local_state)),
    )
    incoming = prefix_state + prefix_decay[:, None, None] * ssm_state
    carried = jnp.exp(cumulative)[:, :, None] * jnp.einsum(
        "tjn,jpn->tjp", c_heads, incoming, precision=highest
    )
    y_heads = local_out + carried + d_skip[None, :, None] * x_heads
    gated = y_heads * jax.nn.silu(gate_z.astype(jnp.float32)).reshape(
        tokens_here, heads_local, head_size
    )
    head_squares = jnp.sum(gated * gated, axis=2)
    if per_group <= heads_local:
        group_sums = jnp.sum(
            head_squares.reshape(tokens_here, heads_local // per_group, per_group), axis=2
        )
        head_mean = jnp.repeat(group_sums, per_group, axis=1) / (per_group * head_size)
    else:
        partial_squares = jnp.sum(head_squares, axis=1, keepdims=True)
        for bit_number in range((per_group // heads_local).bit_length() - 1):
            partial_squares = partial_squares + swapped(partial_squares, "row", bit_number)
        head_mean = jnp.broadcast_to(partial_squares, (tokens_here, heads_local)) / (
            per_group * head_size
        )
    normed = gated * lax.rsqrt(head_mean + 1e-05)[:, :, None]
    y_normed = (normed.reshape(tokens_here, channels) * norm_gain[None, :]).astype(jnp.bfloat16)
    all_tokens = lax.all_gather(y_normed, "col", axis=0, tiled=True)
    return lax.psum_scatter(
        jnp.dot(all_tokens, w_output, preferred_element_type=jnp.float32).astype(jnp.bfloat16),
        "row",
        scatter_dimension=0,
        tiled=True,
    )


def scan_kernel(x_ref, b_ref, c_ref, dt_ref, cum_ref, dt_t_ref, cum_t_ref, skip_ref, first_ref, y_ref, state):
    heads = dt_ref.shape[1]
    size = x_ref.shape[1] // heads
    length = x_ref.shape[0]

    @pl.when(pl.program_id(0) == 0)
    def _():
        state[...] = first_ref[...]

    b = b_ref[...]
    c = c_ref[...]
    contract_last = (((1,), (1,)), ((), ()))
    scores = lax.dot_general(c, b, contract_last, preferred_element_type=jnp.float32)
    rows = lax.broadcasted_iota(jnp.int32, (length, length), 0)
    cols = lax.broadcasted_iota(jnp.int32, (length, length), 1)
    causal = rows >= cols
    scores = jnp.where(causal, scores, 0.0)
    carried = lax.dot_general(
        c, state[...].astype(jnp.bfloat16), contract_last, preferred_element_type=jnp.float32
    )
    outs = []
    weighted = []
    for h in range(heads):
        at = slice(h * size, (h + 1) * size)
        x = x_ref[:, at]
        xf = x.astype(jnp.float32)
        cum = cum_ref[:, h : h + 1]
        cum_t = cum_t_ref[h : h + 1, :]
        last = cum_t[:, length - 1 : length]
        mixing = scores * jnp.exp(jnp.minimum(cum - cum_t, 0.0)) * dt_t_ref[h : h + 1, :]
        intra = jnp.dot(mixing.astype(jnp.bfloat16), x, preferred_element_type=jnp.float32)
        outs.append(
            intra + jnp.exp(cum) * carried[:, at] + skip_ref[h : h + 1, 0:1] * xf
        )
        weighted.append((xf * (jnp.exp(last - cum) * dt_ref[:, h : h + 1])).astype(jnp.bfloat16))
    for h in range(0, heads, 2):
        y_ref[:, h * size : (h + 2) * size] = jnp.concatenate(outs[h : h + 2], axis=1)
    added = lax.dot_general(
        jnp.concatenate(weighted, axis=1),
        b,
        (((0,), (0,)), ((), ())),
        preferred_element_type=jnp.float32,
    )
    for h in range(heads):
        at = slice(h * size, (h + 1) * size)
        decay = jnp.exp(cum_t_ref[h : h + 1, length - 1 : length])
        state[at, :] = decay * state[at, :] + added[at, :]


def scan_heads(x, b, c, dt_t, cum_t, skip, first, block):
    tokens, width = x.shape
    heads, n = dt_t.shape[0], b.shape[1]
    by_rows = lambda w: pl.BlockSpec((block, w), lambda i: (i, 0))
    by_cols = pl.BlockSpec((heads, block), lambda i: (0, i))
    return pl.pallas_call(
        scan_kernel,
        grid=(tokens // block,),
        in_specs=[
            by_rows(width),
            by_rows(n),
            by_rows(n),
            by_rows(heads),
            by_rows(heads),
            by_cols,
            by_cols,
            pl.BlockSpec((heads, 128), lambda i: (0, 0)),
            pl.BlockSpec((width, n), lambda i: (0, 0)),
        ],
        out_specs=by_rows(width),
        out_shape=jax.ShapeDtypeStruct((tokens, width), jnp.float32),
        scratch_shapes=[pltpu.VMEM((width, n), jnp.float32)],
        compiler_params=pltpu.CompilerParams(vmem_limit_bytes=40 * 2**20),
        cost_estimate=pl.CostEstimate(
            flops=2 * tokens * (block * width + 2 * width * n),
            bytes_accessed=8 * tokens * width,
            transcendentals=tokens * block * heads,
        ),
    )(x, b, c, dt_t.T, cum_t.T, dt_t, cum_t, jnp.broadcast_to(skip[:, None], (heads, 128)), first)


def scatter_begin(partial, dim, crossed=False):
    mine = lax.axis_index("col")
    core, chip = mine % 2, mine // 2
    step = partial.shape[dim] // 4

    def block(k, on_core):
        at = on_core * 2 + k if crossed else k * 2 + on_core
        return lax.dynamic_slice_in_dim(partial, at * step, step, dim)

    give = [block(k, 1 - core) for k in range(2)]
    keep = [block(k, core) for k in range(2)]
    got = swapped(jnp.concatenate(give, axis=dim), "col", 0)
    got = [lax.slice_in_dim(got, k * step, (k + 1) * step, axis=dim) for k in range(2)]
    pair = [a.astype(jnp.float32) + b.astype(jnp.float32) for a, b in zip(keep, got)]
    far = jnp.where(chip == 0, pair[1], pair[0]).astype(jnp.bfloat16)
    near = jnp.where(chip == 0, pair[0], pair[1]).astype(jnp.bfloat16)
    return near, far


def scatter_end(near, far):
    return near.astype(jnp.float32) + swapped(far, "col", 1).astype(jnp.float32)


def by_heads(
    hidden,
    w_gate_z,
    w_input_x,
    w_input_bc,
    w_input_dt,
    conv_kernel_x,
    conv_kernel_bc,
    conv_state_x,
    conv_state_bc,
    dt_bias,
    a_log,
    d_skip,
    norm_gain,
    ssm_state,
    w_output,
):
    row, col = lax.axis_index("row"), lax.axis_index("col")
    cols = lax.axis_size("col")
    rows = lax.axis_size("row")
    channels = w_gate_z.shape[1] // cols
    bc_width = w_input_bc.shape[1] // cols
    heads = w_input_dt.shape[1] // cols
    head_size, state_size = ssm_state.shape[1:]

    core, chip = col % 2, col // 2

    def share(array, dim, at=col):
        width = array.shape[dim] // cols
        return lax.dynamic_slice_in_dim(array, at * width, width, dim)

    half = hidden.shape[0] // 2
    halves = [
        lax.all_gather(hidden[i * half : (i + 1) * half], "row", axis=0, tiled=True)
        for i in range(2)
    ]
    length = hidden.shape[0] * rows

    def joined(parts, dim=0):
        shape = parts[0].shape
        cut = shape[:dim] + (rows, half) + shape[dim + 1 :]
        whole = jnp.stack([part.reshape(cut) for part in parts], axis=dim + 1)
        return whole.reshape(shape[:dim] + (length,) + shape[dim + 1 :])

    def picked(array, i):
        cut = array.reshape((rows, 2, half) + array.shape[1:])
        return cut[:, i].reshape((rows * half,) + array.shape[1:])

    def project(tokens, weights):
        return jnp.dot(tokens, weights, preferred_element_type=jnp.float32).astype(jnp.bfloat16)

    def project_all(tokens):
        part_dt = lax.dot_general(
            w_input_dt, tokens, (((0,), (1,)), ((), ())), preferred_element_type=jnp.float32
        ).astype(jnp.bfloat16)
        started_bc = scatter_begin(project(tokens, w_input_bc), 1, crossed=True)
        started_x = scatter_begin(project(tokens, w_input_x), 1)
        started_z = scatter_begin(project(tokens, w_gate_z), 1)
        return part_dt, started_bc, started_x, started_z

    dt_0, bc_0, x_0, z_0 = project_all(halves[0])
    second, bc_0, x_0 = lax.optimization_barrier((halves[1], bc_0, x_0))
    dt_1, bc_1, x_1, z_1 = project_all(second)
    dt_raw = scatter_end(*scatter_begin(joined((dt_0, dt_1), 1), 0))
    input_bc = joined([scatter_end(*part).astype(jnp.bfloat16) for part in (bc_0, bc_1)])
    input_x = joined([scatter_end(*part).astype(jnp.bfloat16) for part in (x_0, x_1)])
    gate_z = joined([scatter_end(*part).astype(jnp.bfloat16) for part in (z_0, z_1)])

    bc_block = core * 2 + chip
    conv_bc = convolve_silu(
        share(conv_state_bc, 1, bc_block), input_bc, share(conv_kernel_bc, 1, bc_block)
    )
    routes = []
    for r in range(rows):
        for c in range(cols):
            group = (r * cols + c) // 2
            from_row = group // cols + (c % 2) * (rows // 2)
            from_col = (group % 2) * 2 + (group % cols) // 2
            routes.append((from_row * cols + from_col, r * cols + c))
    own = lax.ppermute(conv_bc, ("row", "col"), routes)
    other = swapped(own, "col", 0)
    even = col % 2 == 0
    b = jnp.where(even, own, other)
    c = jnp.where(even, other, own)

    block = 256
    steps_dt = jax.nn.softplus(dt_raw + share(dt_bias, 0)[:, None])
    log_decay = steps_dt * (-jnp.exp(share(a_log, 0)))[:, None]
    upper = (jnp.arange(block)[:, None] <= jnp.arange(block)[None, :]).astype(jnp.float32)
    cum = jnp.einsum(
        "hks,st->hkt", log_decay.reshape(heads, length // block, block), upper, precision=highest
    ).reshape(heads, length)
    conv_x = convolve_silu(share(conv_state_x, 1), input_x, share(conv_kernel_x, 1))
    first = share(ssm_state, 0).reshape(heads * head_size, state_size)
    y = scan_heads(conv_x, b, c, steps_dt, cum, share(d_skip, 0), first, block)

    gated = y * jax.nn.silu(gate_z.astype(jnp.float32))
    squares = jnp.sum(gated * gated, axis=1)
    squares = squares + swapped(squares, "col", 0)
    scale = lax.rsqrt(squares / (2 * channels) + 1e-05)
    normed = (gated * scale[:, None] * share(norm_gain, 0)[None, :]).astype(jnp.bfloat16)

    def side_by_side(mine, partner):
        return jnp.where(
            core == 0,
            jnp.concatenate([mine, partner], axis=1),
            jnp.concatenate([partner, mine], axis=1),
        )

    def out_rows(on_chip):
        return lax.dynamic_slice_in_dim(w_output, on_chip * 2 * channels, 2 * channels, 0)

    results = []
    for i in range(2):
        part = picked(normed, i)
        across = swapped(part, "col", 1)
        total = jnp.dot(
            side_by_side(part, swapped(part, "col", 0)),
            out_rows(chip),
            preferred_element_type=jnp.float32,
        )
        across, total = lax.optimization_barrier((across, total))
        total = total + jnp.dot(
            side_by_side(across, swapped(across, "col", 0)),
            out_rows(1 - chip),
            preferred_element_type=jnp.float32,
        )
        results.append(
            lax.psum_scatter(
                total.astype(jnp.bfloat16), "row", scatter_dimension=0, tiled=True
            )
        )
    return jnp.concatenate(results, axis=0)


def local(*arrays):
    w_gate_z, w_input_bc, w_input_dt, ssm_state = arrays[1], arrays[3], arrays[4], arrays[13]
    rows, cols = lax.axis_size("row"), lax.axis_size("col")
    tokens = arrays[0].shape[0] * rows
    state_size = ssm_state.shape[2]
    groups = w_input_bc.shape[1] * rows // (2 * state_size)
    fits = (
        cols == 4
        and w_input_bc.shape[1] == cols * state_size
        and groups * 2 == rows * cols
        and w_input_dt.shape[1] % (2 * cols) == 0
        and w_gate_z.shape[1] % (cols * 128) == 0
        and tokens % 256 == 0
        and arrays[0].shape[0] % 32 == 0
    )
    return by_heads(*arrays) if fits else general(*arrays)


def solution(mesh):
    return jax.shard_map(
        local,
        mesh=mesh,
        in_specs=(
            P(("groups", "row"), "col"),
            P("col", "row"),
            P("col", "row"),
            P("col", "row"),
            P("col", "row"),
            P(None, "row"),
            P(None, "row"),
            P("groups", "row"),
            P("groups", "row"),
            P("row"),
            P("row"),
            P("row"),
            P("row"),
            P(("groups", "row"), None, None),
            P("row", "col"),
        ),
        out_specs=P(("groups", "row"), "col"),
        check_vma=False,
    )
```

```python
import jax
import jax.numpy as jnp
from jax import lax
from jax.experimental import pallas as pl
from jax.experimental.pallas import tpu as pltpu
from jax.sharding import PartitionSpec as P

highest = lax.Precision.HIGHEST


def from_behind(value, axis, steps):
    count = lax.axis_size(axis)
    first, last = (max(0, -steps), min(count, count - steps))
    return lax.ppermute(value, axis, [(source, source + steps) for source in range(first, last)])


def entering(value, axis, combine, identity):
    count, mine = (lax.axis_size(axis), lax.axis_index(axis))
    everything = jax.tree.map(
        lambda part, kind: lax.all_gather(part.astype(kind), axis),
        value,
        (jnp.bfloat16, jnp.bfloat16),
    )
    start = jax.tree.map(
        lambda part, zero: jnp.broadcast_to(jnp.asarray(zero, part.dtype), part.shape),
        value,
        identity,
    )

    def turn(k, before):
        reached = k < mine
        new = combine(
            before, jax.tree.map(lambda part, own: part[k].astype(own.dtype), everything, value)
        )
        return jax.tree.map(lambda a, b: jnp.where(reached, a, b), new, before)

    return lax.fori_loop(0, count, turn, start)


def swapped(value, axis, bit):
    mask = 2**bit
    pairs = [(source, source ^ mask) for source in range(lax.axis_size(axis))]
    return lax.ppermute(value, axis, pairs)


def convolve_silu(previous, current, kernel):
    stacked = jnp.concatenate([previous, current], axis=0).astype(jnp.float32)
    length = current.shape[0]
    accum = jnp.zeros(current.shape, jnp.float32)
    for offset in range(kernel.shape[0]):
        accum = (
            accum + kernel[offset].astype(jnp.float32)[None, :] * stacked[offset : offset + length]
        )
    return jax.nn.silu(accum).astype(jnp.bfloat16)


def block_parts(x_block, b_block, c_block, dt_block, log_block):
    length = x_block.shape[0]
    cumulative = jnp.cumsum(log_block, axis=0)
    scores = jnp.einsum("tjn,sjn->jts", c_block, b_block, precision=highest)
    spans = cumulative.T[:, :, None] - cumulative.T[:, None, :]
    causal = (jnp.arange(length)[:, None] >= jnp.arange(length)[None, :])[None, :, :]
    decay_mask = jnp.where(causal, jnp.exp(jnp.where(causal, spans, 0.0)), 0.0)
    mixing = scores * decay_mask * dt_block.T[:, None, :]
    intra = jnp.einsum("jts,sjp->tjp", mixing, x_block, precision=highest)
    tail_weight = jnp.exp(cumulative[-1][None, :] - cumulative) * dt_block
    local_state = jnp.einsum("sj,sjp,sjn->jpn", tail_weight, x_block, b_block, precision=highest)
    return (intra, cumulative, local_state)


def local_scan(x_heads, b_heads, c_heads, steps_dt, log_decay):
    length, heads_here, head_size = x_heads.shape
    state_size = b_heads.shape[2]
    block_len = min(length, 256)
    blocks = length // block_len

    def to_blocks(array):
        return array.reshape((blocks, block_len) + array.shape[1:])

    def advance(carry_state, inputs):
        x_block, b_block, c_block, dt_block, log_block = inputs
        intra, cumulative, local_state = block_parts(x_block, b_block, c_block, dt_block, log_block)
        carried = jnp.exp(cumulative)[:, :, None] * jnp.einsum(
            "tjn,jpn->tjp", c_block, carry_state, precision=highest
        )
        new_state = jnp.exp(cumulative[-1])[:, None, None] * carry_state + local_state
        return (new_state, intra + carried)

    initial = jnp.zeros((heads_here, head_size, state_size), jnp.float32)
    final_state, outputs = lax.scan(
        advance,
        initial,
        (
            to_blocks(x_heads),
            to_blocks(b_heads),
            to_blocks(c_heads),
            to_blocks(steps_dt),
            to_blocks(log_decay),
        ),
    )
    return (outputs.reshape(length, heads_here, head_size), final_state)


def chain_combine(earlier, later_part):
    return (earlier[0] * later_part[0], later_part[0][:, None, None] * earlier[1] + later_part[1])


def general(
    hidden,
    w_gate_z,
    w_input_x,
    w_input_bc,
    w_input_dt,
    conv_kernel_x,
    conv_kernel_bc,
    conv_state_x,
    conv_state_bc,
    dt_bias,
    a_log,
    d_skip,
    norm_gain,
    ssm_state,
    w_output,
):
    channels = w_gate_z.shape[1]
    bc_local = w_input_bc.shape[1]
    heads_local = w_input_dt.shape[1]
    head_size = ssm_state.shape[1]
    state_size = ssm_state.shape[2]
    kernel_len = conv_kernel_x.shape[0]
    weights = jnp.concatenate([w_gate_z, w_input_x, w_input_bc, w_input_dt], axis=1)
    partial_proj = jnp.dot(
        lax.all_gather(hidden, "row", axis=0, tiled=True),
        weights,
        preferred_element_type=jnp.float32,
    )
    summed = lax.psum_scatter(
        partial_proj.astype(jnp.bfloat16), "col", scatter_dimension=0, tiled=True
    ).astype(jnp.float32)
    gate_z = summed[:, :channels].astype(jnp.bfloat16)
    input_x = summed[:, channels : 2 * channels].astype(jnp.bfloat16)
    input_bc = summed[:, 2 * channels : 2 * channels + bc_local].astype(jnp.bfloat16)
    dt_raw = summed[:, 2 * channels + bc_local :]
    tail_rows = jnp.concatenate(
        [input_x[-(kernel_len - 1) :], input_bc[-(kernel_len - 1) :]], axis=1
    )
    arrived = from_behind(tail_rows, "col", 1)
    first_col = lax.axis_index("col") == 0
    prev_x = jnp.where(first_col, conv_state_x, arrived[:, :channels])
    prev_bc = jnp.where(first_col, conv_state_bc, arrived[:, channels:])
    conv_x = convolve_silu(prev_x, input_x, conv_kernel_x)
    conv_bc = convolve_silu(prev_bc, input_bc, conv_kernel_bc)
    tokens_here = conv_x.shape[0]
    gathered_bc = lax.all_gather(conv_bc, "row", axis=1, tiled=True)
    bc_total = gathered_bc.shape[1]
    group_count = bc_total // (2 * state_size)
    heads_total = heads_local * lax.axis_size("row")
    per_group = heads_total // group_count
    head_ids = lax.axis_index("row") * heads_local + jnp.arange(heads_local, dtype=jnp.int32)
    group_ids = head_ids // per_group
    onehot = group_ids[:, None] == jnp.arange(group_count, dtype=jnp.int32)[None, :]
    b_groups = gathered_bc[:, : bc_total // 2].reshape(tokens_here, group_count, state_size)
    c_groups = gathered_bc[:, bc_total // 2 :].reshape(tokens_here, group_count, state_size)
    b_heads = jnp.einsum(
        "tgn,jg->tjn", b_groups, onehot.astype(jnp.bfloat16), preferred_element_type=jnp.float32
    )
    c_heads = jnp.einsum(
        "tgn,jg->tjn", c_groups, onehot.astype(jnp.bfloat16), preferred_element_type=jnp.float32
    )
    steps_dt = jax.nn.softplus(dt_raw + dt_bias[None, :])
    log_decay = steps_dt * (-jnp.exp(a_log))[None, :]
    x_heads = conv_x.astype(jnp.float32).reshape(tokens_here, heads_local, head_size)
    local_out, local_state = local_scan(x_heads, b_heads, c_heads, steps_dt, log_decay)
    cumulative = jnp.cumsum(log_decay, axis=0)
    decay_total = jnp.exp(cumulative[-1])
    prefix_decay, prefix_state = entering(
        (decay_total, local_state),
        "col",
        chain_combine,
        (jnp.ones_like(decay_total), jnp.zeros_like(local_state)),
    )
    incoming = prefix_state + prefix_decay[:, None, None] * ssm_state
    carried = jnp.exp(cumulative)[:, :, None] * jnp.einsum(
        "tjn,jpn->tjp", c_heads, incoming, precision=highest
    )
    y_heads = local_out + carried + d_skip[None, :, None] * x_heads
    gated = y_heads * jax.nn.silu(gate_z.astype(jnp.float32)).reshape(
        tokens_here, heads_local, head_size
    )
    head_squares = jnp.sum(gated * gated, axis=2)
    if per_group <= heads_local:
        group_sums = jnp.sum(
            head_squares.reshape(tokens_here, heads_local // per_group, per_group), axis=2
        )
        head_mean = jnp.repeat(group_sums, per_group, axis=1) / (per_group * head_size)
    else:
        partial_squares = jnp.sum(head_squares, axis=1, keepdims=True)
        for bit_number in range((per_group // heads_local).bit_length() - 1):
            partial_squares = partial_squares + swapped(partial_squares, "row", bit_number)
        head_mean = jnp.broadcast_to(partial_squares, (tokens_here, heads_local)) / (
            per_group * head_size
        )
    normed = gated * lax.rsqrt(head_mean + 1e-05)[:, :, None]
    y_normed = (normed.reshape(tokens_here, channels) * norm_gain[None, :]).astype(jnp.bfloat16)
    all_tokens = lax.all_gather(y_normed, "col", axis=0, tiled=True)
    return lax.psum_scatter(
        jnp.dot(all_tokens, w_output, preferred_element_type=jnp.float32).astype(jnp.bfloat16),
        "row",
        scatter_dimension=0,
        tiled=True,
    )


def scan_kernel(x_ref, b_ref, c_ref, dt_ref, cum_ref, dt_t_ref, cum_t_ref, skip_ref, first_ref, y_ref, state):
    heads = dt_ref.shape[1]
    size = x_ref.shape[1] // heads
    length = x_ref.shape[0]

    @pl.when(pl.program_id(0) == 0)
    def _():
        state[...] = first_ref[...]

    b = b_ref[...]
    c = c_ref[...]
    contract_last = (((1,), (1,)), ((), ()))
    scores = lax.dot_general(c, b, contract_last, preferred_element_type=jnp.float32)
    rows = lax.broadcasted_iota(jnp.int32, (length, length), 0)
    cols = lax.broadcasted_iota(jnp.int32, (length, length), 1)
    causal = rows >= cols
    scores = jnp.where(causal, scores, 0.0)
    carried = lax.dot_general(
        c, state[...].astype(jnp.bfloat16), contract_last, preferred_element_type=jnp.float32
    )
    outs = []
    weighted = []
    for h in range(heads):
        at = slice(h * size, (h + 1) * size)
        x = x_ref[:, at]
        xf = x.astype(jnp.float32)
        cum = cum_ref[:, h : h + 1]
        cum_t = cum_t_ref[h : h + 1, :]
        last = cum_t[:, length - 1 : length]
        mixing = scores * jnp.exp(jnp.minimum(cum - cum_t, 0.0)) * dt_t_ref[h : h + 1, :]
        intra = jnp.dot(mixing.astype(jnp.bfloat16), x, preferred_element_type=jnp.float32)
        outs.append(
            intra + jnp.exp(cum) * carried[:, at] + skip_ref[h : h + 1, 0:1] * xf
        )
        weighted.append((xf * (jnp.exp(last - cum) * dt_ref[:, h : h + 1])).astype(jnp.bfloat16))
    for h in range(0, heads, 2):
        y_ref[:, h * size : (h + 2) * size] = jnp.concatenate(outs[h : h + 2], axis=1)
    added = lax.dot_general(
        jnp.concatenate(weighted, axis=1),
        b,
        (((0,), (0,)), ((), ())),
        preferred_element_type=jnp.float32,
    )
    for h in range(heads):
        at = slice(h * size, (h + 1) * size)
        decay = jnp.exp(cum_t_ref[h : h + 1, length - 1 : length])
        state[at, :] = decay * state[at, :] + added[at, :]


def scan_heads(x, b, c, dt_t, cum_t, skip, first, block):
    tokens, width = x.shape
    heads, n = dt_t.shape[0], b.shape[1]
    by_rows = lambda w: pl.BlockSpec((block, w), lambda i: (i, 0))
    by_cols = pl.BlockSpec((heads, block), lambda i: (0, i))
    return pl.pallas_call(
        scan_kernel,
        grid=(tokens // block,),
        in_specs=[
            by_rows(width),
            by_rows(n),
            by_rows(n),
            by_rows(heads),
            by_rows(heads),
            by_cols,
            by_cols,
            pl.BlockSpec((heads, 128), lambda i: (0, 0)),
            pl.BlockSpec((width, n), lambda i: (0, 0)),
        ],
        out_specs=by_rows(width),
        out_shape=jax.ShapeDtypeStruct((tokens, width), jnp.float32),
        scratch_shapes=[pltpu.VMEM((width, n), jnp.float32)],
        compiler_params=pltpu.CompilerParams(vmem_limit_bytes=40 * 2**20),
        cost_estimate=pl.CostEstimate(
            flops=2 * tokens * (block * width + 2 * width * n),
            bytes_accessed=8 * tokens * width,
            transcendentals=tokens * block * heads,
        ),
    )(x, b, c, dt_t.T, cum_t.T, dt_t, cum_t, jnp.broadcast_to(skip[:, None], (heads, 128)), first)


def scatter_begin(partial, dim, crossed=False):
    mine = lax.axis_index("col")
    core, chip = mine % 2, mine // 2
    step = partial.shape[dim] // 4

    def block(k, on_core):
        at = on_core * 2 + k if crossed else k * 2 + on_core
        return lax.dynamic_slice_in_dim(partial, at * step, step, dim)

    give = [block(k, 1 - core) for k in range(2)]
    keep = [block(k, core) for k in range(2)]
    got = swapped(jnp.concatenate(give, axis=dim), "col", 0)
    got = [lax.slice_in_dim(got, k * step, (k + 1) * step, axis=dim) for k in range(2)]
    pair = [a.astype(jnp.float32) + b.astype(jnp.float32) for a, b in zip(keep, got)]
    far = jnp.where(chip == 0, pair[1], pair[0]).astype(jnp.bfloat16)
    near = jnp.where(chip == 0, pair[0], pair[1]).astype(jnp.bfloat16)
    return near, far


def scatter_end(near, far):
    return near.astype(jnp.float32) + swapped(far, "col", 1).astype(jnp.float32)


def by_heads(
    hidden,
    w_gate_z,
    w_input_x,
    w_input_bc,
    w_input_dt,
    conv_kernel_x,
    conv_kernel_bc,
    conv_state_x,
    conv_state_bc,
    dt_bias,
    a_log,
    d_skip,
    norm_gain,
    ssm_state,
    w_output,
):
    row, col = lax.axis_index("row"), lax.axis_index("col")
    cols = lax.axis_size("col")
    rows = lax.axis_size("row")
    channels = w_gate_z.shape[1] // cols
    bc_width = w_input_bc.shape[1] // cols
    heads = w_input_dt.shape[1] // cols
    head_size, state_size = ssm_state.shape[1:]

    core, chip = col % 2, col // 2

    def share(array, dim, at=col):
        width = array.shape[dim] // cols
        return lax.dynamic_slice_in_dim(array, at * width, width, dim)

    half = hidden.shape[0] // 2
    halves = [
        lax.all_gather(hidden[i * half : (i + 1) * half], "row", axis=0, tiled=True)
        for i in range(2)
    ]
    length = hidden.shape[0] * rows

    def joined(parts, dim=0):
        shape = parts[0].shape
        cut = shape[:dim] + (rows, half) + shape[dim + 1 :]
        whole = jnp.stack([part.reshape(cut) for part in parts], axis=dim + 1)
        return whole.reshape(shape[:dim] + (length,) + shape[dim + 1 :])

    def picked(array, i):
        cut = array.reshape((rows, 2, half) + array.shape[1:])
        return cut[:, i].reshape((rows * half,) + array.shape[1:])

    def project(tokens, weights):
        return jnp.dot(tokens, weights, preferred_element_type=jnp.float32).astype(jnp.bfloat16)

    def project_dt(tokens):
        return lax.dot_general(
            w_input_dt, tokens, (((0,), (1,)), ((), ())), preferred_element_type=jnp.float32
        ).astype(jnp.bfloat16)

    def across_chips(far):
        return swapped(far, "col", 1)

    def total(near, received):
        return (near.astype(jnp.float32) + received.astype(jnp.float32)).astype(jnp.bfloat16)

    first_half, second_half = halves
    near_bc_0, far = scatter_begin(project(first_half, w_input_bc), 1, crossed=True)
    got_bc_0 = across_chips(far)
    near_x_0, far = scatter_begin(project(first_half, w_input_x), 1)
    got_x_0 = across_chips(far)
    dt_0 = project_dt(first_half)
    near_z_0, far = scatter_begin(project(first_half, w_gate_z), 1)
    second_half, got_bc_0 = lax.optimization_barrier((second_half, got_bc_0))
    dt_1 = project_dt(second_half)
    near_bc_1, far_bc_1 = scatter_begin(project(second_half, w_input_bc), 1, crossed=True)
    near_x_1, far_x_1 = scatter_begin(project(second_half, w_input_x), 1)
    second_half, far, got_x_0 = lax.optimization_barrier((second_half, far, got_x_0))
    got_z_0 = across_chips(far)
    near_z_1, far_z_1 = scatter_begin(project(second_half, w_gate_z), 1)
    got_bc_1 = across_chips(far_bc_1)
    far_x_1, got_z_0 = lax.optimization_barrier((far_x_1, got_z_0))
    got_x_1 = across_chips(far_x_1)
    far_z_1, got_x_1 = lax.optimization_barrier((far_z_1, got_x_1))
    got_z_1 = across_chips(far_z_1)
    dt_raw = scatter_end(*scatter_begin(joined((dt_0, dt_1), 1), 0))
    input_bc = joined((total(near_bc_0, got_bc_0), total(near_bc_1, got_bc_1)))
    input_x = joined((total(near_x_0, got_x_0), total(near_x_1, got_x_1)))
    gate_z = joined((total(near_z_0, got_z_0), total(near_z_1, got_z_1)))

    bc_block = core * 2 + chip
    conv_bc = convolve_silu(
        share(conv_state_bc, 1, bc_block), input_bc, share(conv_kernel_bc, 1, bc_block)
    )
    routes = []
    for r in range(rows):
        for c in range(cols):
            group = (r * cols + c) // 2
            from_row = group // cols + (c % 2) * (rows // 2)
            from_col = (group % 2) * 2 + (group % cols) // 2
            routes.append((from_row * cols + from_col, r * cols + c))
    own = lax.ppermute(conv_bc, ("row", "col"), routes)
    other = swapped(own, "col", 0)
    even = col % 2 == 0
    b = jnp.where(even, own, other)
    c = jnp.where(even, other, own)

    block = 256
    steps_dt = jax.nn.softplus(dt_raw + share(dt_bias, 0)[:, None])
    log_decay = steps_dt * (-jnp.exp(share(a_log, 0)))[:, None]
    upper = (jnp.arange(block)[:, None] <= jnp.arange(block)[None, :]).astype(jnp.float32)
    cum = jnp.einsum(
        "hks,st->hkt", log_decay.reshape(heads, length // block, block), upper, precision=highest
    ).reshape(heads, length)
    conv_x = convolve_silu(share(conv_state_x, 1), input_x, share(conv_kernel_x, 1))
    first = share(ssm_state, 0).reshape(heads * head_size, state_size)
    y = scan_heads(conv_x, b, c, steps_dt, cum, share(d_skip, 0), first, block)

    gated = y * jax.nn.silu(gate_z.astype(jnp.float32))
    squares = jnp.sum(gated * gated, axis=1)
    squares = squares + swapped(squares, "col", 0)
    scale = lax.rsqrt(squares / (2 * channels) + 1e-05)
    normed = (gated * scale[:, None] * share(norm_gain, 0)[None, :]).astype(jnp.bfloat16)

    def side_by_side(mine, partner):
        return jnp.where(
            core == 0,
            jnp.concatenate([mine, partner], axis=1),
            jnp.concatenate([partner, mine], axis=1),
        )

    def out_rows(on_chip):
        return lax.dynamic_slice_in_dim(w_output, on_chip * 2 * channels, 2 * channels, 0)

    results = []
    for i in range(2):
        part = picked(normed, i)
        across = swapped(part, "col", 1)
        mixed = jnp.dot(
            side_by_side(part, swapped(part, "col", 0)),
            out_rows(chip),
            preferred_element_type=jnp.float32,
        )
        across, mixed = lax.optimization_barrier((across, mixed))
        mixed = mixed + jnp.dot(
            side_by_side(across, swapped(across, "col", 0)),
            out_rows(1 - chip),
            preferred_element_type=jnp.float32,
        )
        results.append(
            lax.psum_scatter(
                mixed.astype(jnp.bfloat16), "row", scatter_dimension=0, tiled=True
            )
        )
    return jnp.concatenate(results, axis=0)


def local(*arrays):
    w_gate_z, w_input_bc, w_input_dt, ssm_state = arrays[1], arrays[3], arrays[4], arrays[13]
    rows, cols = lax.axis_size("row"), lax.axis_size("col")
    tokens = arrays[0].shape[0] * rows
    state_size = ssm_state.shape[2]
    groups = w_input_bc.shape[1] * rows // (2 * state_size)
    fits = (
        cols == 4
        and w_input_bc.shape[1] == cols * state_size
        and groups * 2 == rows * cols
        and w_input_dt.shape[1] % (2 * cols) == 0
        and w_gate_z.shape[1] % (cols * 128) == 0
        and tokens % 256 == 0
        and arrays[0].shape[0] % 32 == 0
    )
    return by_heads(*arrays) if fits else general(*arrays)


def solution(mesh):
    return jax.shard_map(
        local,
        mesh=mesh,
        in_specs=(
            P(("groups", "row"), "col"),
            P("col", "row"),
            P("col", "row"),
            P("col", "row"),
            P("col", "row"),
            P(None, "row"),
            P(None, "row"),
            P("groups", "row"),
            P("groups", "row"),
            P("row"),
            P("row"),
            P("row"),
            P("row"),
            P(("groups", "row"), None, None),
            P("row", "col"),
        ),
        out_specs=P(("groups", "row"), "col"),
        check_vma=False,
    )
```
